512 devices in a mesh: rep: 64 (over z_lo, y, core), tp: 8 (over x, z_hi).
Axes of the slice: x: 4, y: 4, z: 16 (z_hi: 2, z_lo: 8; z = z_hi * 8 + z_lo), core: 2. Of those that a mesh axis runs over, the one named last changes fastest.
Arguments:
- context: bfloat16 [2, 32768, 2048], P(None, 'rep', 'tp'), may hold values from -6 to 6
- residual: bfloat16 [2, 32768, 2304], P(None, 'rep', 'tp'), may hold values from -40 to 40, as said below
- targets: bfloat16 [2, 32768, 2304], P(None, 'rep', 'tp'), may hold values from -6 to 6
- gain: float32 [2304], P('tp'), may hold values from 0.1 to 1.9
- slow_weight: bfloat16 [2048, 2304], P(None, 'tp'), may hold values from -0.125 to 0.125
- momentum: float32 [2048, 2304], P('rep', 'tp'), may hold values from -4 to 4
- shares: float32 [2, 64], P(None, 'rep'), may hold values from 0.3 to 0.7
Outputs:
- new_weight: float32 [2048, 2304], P('rep', 'tp')
- new_momentum: float32 [2048, 2304], P('rep', 'tp')
- push_mass: float32 [64], P('rep')
The draws below stay inside these ranges and needn't reach their ends.
Inputs may be any that keep to these rules, and one draw needn't show every extreme that they name: `residual`: Real-valued.
All inputs are finite; a program needn't handle non-finite values.
Results may differ from the reference program's by a relative error of at most 0.0045.
Values may be sent and summed in bfloat16 or wider, within the bound.
No kernel may reach another device: no remote copies, remote signals or barrier semaphores. Data moves between devices by JAX's collectives and lax.ppermute only.
A program may use at most 64 MiB of HBM per device.

```python
import jax
import jax.numpy as jnp
from jax import lax

D = 2304
STEPS = 2
TOK = 512
HD_ALL = 2048
REPLICAS = 64
TOKENS = 32768


def draw_residual(key, part):
    key = jax.random.fold_in(key, 11)
    first_key, second_key = jax.random.split(key, 2)
    columns = jnp.arange(D, dtype=jnp.float32) / D
    column_scale = jnp.exp(columns * jnp.log(10.0)) / 3.0
    row_scale = jnp.exp(jax.random.uniform(second_key, (STEPS, TOKENS, 1), jnp.float32, jnp.log(0.3), jnp.log(3.0)))
    noise = jax.random.normal(first_key, (STEPS, TOKENS, D), jnp.float32)
    values = noise * column_scale * row_scale
    return jnp.clip(values, -40.0, 40.0).astype(jnp.bfloat16)


def level_of(rng, dims, cuts, low, largest):
    factor_of, own = 1.0, jax.random.fold_in(rng, 6)
    for dim, parts in cuts:
        heights = jnp.exp(jax.random.uniform(jax.random.fold_in(own, dim), (parts,), jnp.float32, low / len(cuts), largest / len(cuts)))
        factor_of = factor_of * jnp.repeat(heights, dims[dim] // parts).reshape([-1 if axis == dim else 1 for axis in range(len(dims))])
    return factor_of


def normal_values(rng, dims, width, bound, pieces=(), kind=jnp.bfloat16):
    level = level_of(rng, dims, pieces, -0.22, 0.18) if pieces else 1.0
    array = jax.random.normal(rng, dims, jnp.float32) * width * level
    return jnp.minimum(jnp.maximum(array, -bound), bound).astype(kind)


def setup_inputs(seed: int = 0) -> dict:
    key_list = jax.random.split(jax.random.key(seed), 8)
    context = normal_values(key_list[0], (STEPS, TOKENS, HD_ALL), 1.0, 6.0, ((1, 64), (2, 8)))
    residual = draw_residual(jax.random.fold_in(key_list[7], 71), 0)
    targets = normal_values(key_list[2], (STEPS, TOKENS, D), 1.0, 6.0, ((1, 64), (2, 8)))
    gain = jnp.clip(1.0 + 0.18 * jax.random.normal(key_list[3], (D,), jnp.float32), 0.1, 1.9)
    slow_weight = normal_values(key_list[4], (HD_ALL, D), HD_ALL ** -0.5, 0.125, ((1, 8),))
    momentum = normal_values(key_list[5], (HD_ALL, D), 0.5, 4.0, ((0, 64), (1, 8)), jnp.float32)
    shares = jnp.clip(0.3 + 0.39999998 * jax.random.uniform(key_list[6], (STEPS, REPLICAS), jnp.float32) ** level_of(key_list[6], (STEPS, REPLICAS), ((1, 64),), -0.2, 0.2), 0.3, 0.7)
    return dict(context=context, residual=residual, targets=targets, gain=gain, slow_weight=slow_weight, momentum=momentum, shares=shares)


LR = 0.005
BETA = 0.7
ALPHA = 1.0
EPS = 1e-06

def replica_gradient(quotient, context_rows, residual_rows, target_rows, gain):
    scale = TOK ** (-0.5)
    output = residual_rows.astype(jnp.float32) + jnp.dot(context_rows, quotient, preferred_element_type=jnp.float32)
    root_mean = jnp.sqrt(lax.optimization_barrier(jnp.mean(output * output, axis=1, keepdims=True)) + EPS)
    normed = output / root_mean
    normed_grad = scale * gain * (gain * normed - target_rows.astype(jnp.float32))
    projection = lax.optimization_barrier(jnp.mean(normed_grad * normed, axis=1, keepdims=True))
    output_grad = ((normed_grad - normed * projection) / root_mean).astype(jnp.bfloat16)
    return jnp.dot(context_rows.T, output_grad, preferred_element_type=jnp.float32)

def reference(context, residual, targets, gain, slow_weight, momentum, shares):
    anchor = slow_weight.astype(jnp.float32)
    numerator = jnp.broadcast_to(anchor, (REPLICAS,) + anchor.shape)
    push_mass = jnp.ones((REPLICAS,), jnp.float32)
    for step in range(STEPS):
        context_step = context[step].reshape(REPLICAS, TOK, HD_ALL)
        residual_step = residual[step].reshape(REPLICAS, TOK, D)
        target_step = targets[step].reshape(REPLICAS, TOK, D)

        def advance(items):
            values, weight_mass, context_rows, residual_rows, target_rows = items
            quotient = (values / weight_mass).astype(jnp.bfloat16)
            return values - LR * replica_gradient(quotient, context_rows, residual_rows, target_rows, gain)
        stepped = lax.map(advance, (numerator, push_mass, context_step, residual_step, target_step))
        kept_share = shares[step]
        outgoing = ((1.0 - kept_share)[:, None, None] * stepped).astype(jnp.bfloat16)
        numerator = kept_share[:, None, None] * stepped + jnp.roll(outgoing, step + 1, axis=0).astype(jnp.float32)
        push_mass = kept_share * push_mass + jnp.roll((1.0 - kept_share) * push_mass, step + 1)
    average = lax.optimization_barrier(jnp.mean(numerator / push_mass[:, None, None], axis=0))
    new_momentum = BETA * momentum + (anchor - average) / LR
    new_weight = anchor - ALPHA * LR * new_momentum
    return (new_weight, new_momentum, push_mass)
```

```python
import jax
import jax.numpy as jnp
from jax import lax
from jax.sharding import Mesh, PartitionSpec as P

D = 2304
TOK = 512
LR = 0.005
BETA = 0.7
ALPHA = 1.0
EPS = 1e-06
SCALE = TOK ** (-0.5)

AXES = ("z_lo", "y", "core", "x", "z_hi")
SIZES = (8, 4, 2, 4, 2)
REP = AXES[:3]
TP = AXES[3:]
F32 = jnp.float32
BF16 = jnp.bfloat16


def shifted(value, axis, steps):
    count = lax.axis_size(axis)
    return lax.ppermute(value, axis, [(i, (i + steps) % count) for i in range(count)])


def to_all(value, axis):
    count = lax.axis_size(axis)
    return lax.all_to_all(jnp.broadcast_to(value[None], (count,) + value.shape), axis, 0, 0)


def contract_rows(left, right):
    return lax.dot_general(left, right, (((0,), (0,)), ((), ())), preferred_element_type=F32)


def merged(own, other, hi):
    low = jnp.where(hi == 0, own, other)
    high = jnp.where(hi == 0, other, own)
    both = jnp.stack([low, high], axis=1)
    return jnp.transpose(both, (2, 0, 1, 3)).reshape(TOK, 2048)


def forward(gathered, quotient, residual, targets, gain):
    output = residual.astype(F32) + jnp.dot(gathered, quotient, preferred_element_type=F32)
    scaled = gain * output
    sums = jnp.stack(
        [
            jnp.sum(output * output, axis=1),
            jnp.sum(scaled * scaled, axis=1),
            jnp.sum(scaled * targets.astype(F32), axis=1),
        ]
    )
    return output, sums


def backward(output, totals, targets, gain):
    root_sq = totals[0] / D + EPS
    root = jnp.sqrt(root_sq)
    projection = SCALE * (totals[1] / root_sq - totals[2] / root) / D
    normed = output / root[:, None]
    normed_grad = SCALE * gain * (gain * normed - targets.astype(F32))
    return ((normed_grad - normed * projection[:, None]) / root[:, None]).astype(BF16)


def body(context, residual, targets, gain, slow_weight, momentum, shares):
    hi = lax.axis_index("z_hi")
    core = lax.axis_index("core")
    anchor = slow_weight.astype(F32)

    own_share = shares[:, 0]
    before = shifted(own_share, REP, 1)
    after = shifted(own_share, REP, -1)

    other0 = shifted(context[0], "z_hi", 1)
    x_own0 = to_all(context[0], "x")
    other0, x_own0 = lax.optimization_barrier((other0, x_own0))
    other1 = shifted(context[1], "z_hi", 1)
    x_own1 = lax.all_gather(context[1], "x", axis=0)
    x_other0 = to_all(other0, "x")
    gathered0 = merged(x_own0, x_other0, hi)

    output0, sums0 = forward(gathered0, slow_weight, residual[0], targets[0], gain)
    totals0 = jnp.sum(to_all(sums0, TP), axis=0)
    grad0 = backward(output0, totals0, targets[0], gain)
    weight_grad0 = contract_rows(gathered0, grad0)

    incoming = shifted(((1.0 - own_share[0]) * weight_grad0).astype(BF16), REP, 1)
    other1, weight_grad0 = lax.optimization_barrier((other1, weight_grad0))
    x_other1 = to_all(other1, "x")
    window = jnp.stack([before, own_share, after])
    earlier = shifted(window, REP, 2)
    later = shifted(window, REP, -2)
    gathered1 = merged(x_own1, x_other1, hi)

    mass1 = own_share[0] + (1.0 - before[0])
    step0 = own_share[0] * weight_grad0 + incoming.astype(F32)
    quotient1 = (anchor - (LR / mass1) * step0).astype(BF16)
    output1, sums1 = forward(gathered1, quotient1, residual[1], targets[1], gain)
    totals1 = jnp.sum(to_all(sums1, TP), axis=0)
    grad1 = backward(output1, totals1, targets[1], gain)
    weight_grad1 = contract_rows(gathered1, grad1)

    near = jnp.concatenate([earlier[:2], window, later[1:]])
    first = {k: near[k + 3, 0] for k in range(-3, 4)}
    second = {k: near[k + 3, 1] for k in range(-3, 4)}
    mass_of = {k: first[k] + (1.0 - first[k - 1]) for k in range(-2, 4)}
    final_of = {
        k: second[k] * mass_of[k] + (1.0 - second[k - 2]) * mass_of[k - 2] for k in range(0, 4)
    }
    part_of = {k: second[k] / final_of[k] + (1.0 - second[k]) / final_of[k + 2] for k in (0, 1)}
    replicas = lax.axis_size(REP)
    coef1 = part_of[0] / replicas
    coef0 = (part_of[0] * first[0] + part_of[1] * (1.0 - first[0])) / replicas
    total = coef0 * weight_grad0 + coef1 * weight_grad1

    width = total.shape[1]
    total = total.reshape(8, 4, 2, 32, width)
    kept = jnp.where(core == 0, total[:, :, 0], total[:, :, 1])
    sent = jnp.where(core == 0, total[:, :, 1], total[:, :, 0]).astype(BF16)
    total = kept + shifted(sent, "core", 1).astype(F32)
    parts = jnp.transpose(total.astype(BF16), (1, 0, 2, 3))
    parts = lax.all_to_all(parts, "y", 0, 0)
    total = jnp.sum(parts.astype(F32), axis=0)
    parts = lax.all_to_all(total.astype(BF16), "z_lo", 0, 0)
    gradient = jnp.sum(parts.astype(F32), axis=0)

    anchor_rows = lax.dynamic_slice_in_dim(slow_weight, lax.axis_index(REP) * 32, 32, 0)
    new_momentum = BETA * momentum + gradient
    new_weight = anchor_rows.astype(F32) - ALPHA * LR * new_momentum
    return (new_weight, new_momentum, final_of[0][None])


def solution(mesh):
    fine = Mesh(mesh.devices.reshape(SIZES), AXES)
    return jax.shard_map(
        body,
        mesh=fine,
        in_specs=(
            P(None, REP, TP),
            P(None, REP, TP),
            P(None, REP, TP),
            P(TP),
            P(None, TP),
            P(REP, TP),
            P(None, REP),
        ),
        out_specs=(P(REP, TP), P(REP, TP), P(REP)),
        check_vma=False,
    )
```

```python
import jax
import jax.numpy as jnp
from jax import lax
from jax.experimental import pallas as pl
from jax.experimental.pallas import tpu as pltpu
from jax.sharding import Mesh, PartitionSpec as P

D = 2304
TOK = 512
LR = 0.005
BETA = 0.7
ALPHA = 1.0
EPS = 1e-06
SCALE = TOK ** (-0.5)

AXES = ("z_lo", "y", "core", "x", "z_hi")
SIZES = (8, 4, 2, 4, 2)
REP = AXES[:3]
TP = AXES[3:]
F32 = jnp.float32
BF16 = jnp.bfloat16
CHUNK = 256
SMEM = pl.BlockSpec(memory_space=pltpu.SMEM)


def shifted(value, axis, steps):
    count = lax.axis_size(axis)
    return lax.ppermute(value, axis, [(i, (i + steps) % count) for i in range(count)])


def to_all(value, axis):
    count = lax.axis_size(axis)
    return lax.all_to_all(jnp.broadcast_to(value[None], (count,) + value.shape), axis, 0, 0)


def after(value, *others):
    return lax.optimization_barrier((value,) + others)[0]


def call(kernel, specs, out_specs, outs, flops, *args, scratch=(), steps=4):
    size = sum(a.size * a.dtype.itemsize for a in args) + sum(
        o.size * o.dtype.itemsize for o in outs
    )
    return pl.pallas_call(
        kernel,
        grid=(steps,),
        out_shape=outs,
        in_specs=specs,
        out_specs=out_specs,
        scratch_shapes=scratch,
        compiler_params=pltpu.CompilerParams(vmem_limit_bytes=24 * 2**20),
        cost_estimate=pl.CostEstimate(flops=flops, bytes_accessed=size, transcendentals=0),
    )(*args)


def whole(dims):
    return pl.BlockSpec(dims, lambda x: (0,) * len(dims))


def layer(step, dims):
    return pl.BlockSpec((1,) + dims, lambda x: (step, 0, 0))


FEATURES = pl.BlockSpec((1, 2, TOK, CHUNK), lambda x: (x, 0, 0, 0))


def dot(left, right, left_dim, right_dim):
    return lax.dot_general(
        left, right, (((left_dim,), (right_dim,)), ((), ())), preferred_element_type=F32
    )


def columns(hi, other):
    half = 1 - hi if other else hi
    return half, pl.ds(pl.multiple_of(half * CHUNK, CHUNK), CHUNK)


def token_sums(output, gain, targets, sums_ref):
    scaled = gain * output
    rows = [
        jnp.sum(output * output, axis=0, keepdims=True),
        jnp.sum(scaled * scaled, axis=0, keepdims=True),
        jnp.sum(scaled * targets, axis=0, keepdims=True),
        jnp.zeros((5, TOK), F32),
    ]
    block = jnp.concatenate(rows, axis=0)
    for peer in range(sums_ref.shape[0]):
        sums_ref[peer] = block


def first_forward(place_ref, both_ref, weight_ref, res_ref, tgt_ref, gain_ref, out_ref, sums_ref):
    x = pl.program_id(0)

    @pl.when(x == 0)
    def _():
        out_ref[...] = res_ref[0].astype(F32)

    acc = out_ref[...]
    for other in range(2):
        _, cols = columns(place_ref[0], other)
        acc += dot(weight_ref[:, cols], both_ref[0, other], 1, 1)
    out_ref[...] = acc

    @pl.when(x == 3)
    def _():
        token_sums(out_ref[...], gain_ref[...], tgt_ref[0].astype(F32), sums_ref)


def output_gradient(recv_ref, out_ref, tgt_ref, gain_ref):
    totals = recv_ref[0]
    for peer in range(1, recv_ref.shape[0]):
        totals += recv_ref[peer]
    root_sq = totals[0:1] / D + EPS
    root = jnp.sqrt(root_sq)
    projection = SCALE * (totals[1:2] / root_sq - totals[2:3] / root) / D
    gain = gain_ref[...]
    normed = out_ref[...] / root
    normed_grad = SCALE * gain * (gain * normed - tgt_ref[0].astype(F32))
    return (normed_grad - normed * projection) / root


def first_backward(recv_ref, out_ref, tgt_ref, gain_ref, share_ref, kept_ref, sent_ref):
    grad = output_gradient(recv_ref, out_ref, tgt_ref, gain_ref)
    share = share_ref[...]
    kept_ref[...] = (share * grad).astype(BF16)
    sent_ref[...] = ((1.0 - share) * grad).astype(BF16)


def second_forward(
    place_ref, both_ref, prev_ref, next_ref, kept_ref, recv_ref, weight_ref, res_ref, tgt_ref,
    gain_ref, mass_ref, out_ref, sums_ref,
):
    x = pl.program_id(0)

    @pl.when(x == 0)
    def _():
        out_ref[...] = res_ref[0].astype(F32)

    factor = LR / mass_ref[:, :CHUNK]
    acc = out_ref[...]
    for other in range(2):
        _, cols = columns(place_ref[0], other)
        move = dot(kept_ref[...], both_ref[0, other], 1, 0)
        move += dot(recv_ref[...], prev_ref[0, other], 1, 0)
        quotient = (weight_ref[:, cols].astype(F32) - factor * move).astype(BF16)
        acc += dot(quotient, next_ref[0, other], 1, 1)
    out_ref[...] = acc

    @pl.when(x == 3)
    def _():
        token_sums(out_ref[...], gain_ref[...], tgt_ref[0].astype(F32), sums_ref)


def first_rows(place_ref, both_ref, prev_ref, kept_ref, recv_ref, rows_ref):
    for other in range(2):
        half, _ = columns(place_ref[0], other)
        rows_ref[half] = dot(both_ref[0, other], kept_ref[...], 0, 1) + dot(
            prev_ref[0, other], recv_ref[...], 0, 1
        )


def second_backward(
    place_ref, recv_ref, out_ref, tgt_ref, gain_ref, coef_ref, next_ref, rows_ref,
    kept_ref, sent_ref, grad_ref, total_ref,
):
    hi, core = place_ref[0], place_ref[1]

    @pl.when(pl.program_id(0) == 0)
    def _():
        grad_ref[...] = output_gradient(recv_ref, out_ref, tgt_ref, gain_ref).astype(BF16)

    coef = coef_ref[:, :288]
    for other in range(2):
        half, _ = columns(hi, other)
        total_ref[...] = coef * (rows_ref[half] + dot(next_ref[0, other], grad_ref[...], 0, 1))
        for y in range(4):
            mine = pl.ds(pl.multiple_of((2 * y + core) * 32, 32), 32)
            away = pl.ds(pl.multiple_of((2 * y + 1 - core) * 32, 32), 32)
            kept_ref[y, half] = total_ref[mine, :]
            sent_ref[y, half] = total_ref[away, :].astype(BF16)


def shape(dims, dtype):
    return jax.ShapeDtypeStruct(dims, dtype)


def body(context, residual, targets, gain, slow_weight, momentum, shares):
    hi = lax.axis_index("z_hi").astype(jnp.int32)
    core = lax.axis_index("core").astype(jnp.int32)
    place = jnp.stack([hi, core])
    weight = slow_weight.T
    res = jnp.transpose(residual, (0, 2, 1))
    tgt = jnp.transpose(targets, (0, 2, 1))
    gain = gain[:, None]
    width = weight.shape[0]
    share0 = jnp.broadcast_to(shares[0:1], (1, TOK))
    share1 = jnp.broadcast_to(shares[1:2], (1, TOK))

    out, sums, pair = whole((width, TOK)), whole((8, 8, TOK)), whole((width, TOK))
    col, row = whole((width, 1)), whole((1, TOK))
    wts = pl.BlockSpec((width, 2 * CHUNK), lambda x: (0, x))
    rows_spec = pl.BlockSpec((2, CHUNK, width), lambda x: (x, 0, 0))
    cut = pl.BlockSpec((4, 2, 32, width), lambda x: (0, x, 0, 0))
    flops = 2 * TOK * 2048 * width

    other0 = shifted(context[0], "z_hi", 1)
    context1, share0 = lax.optimization_barrier((context[1], share0, other0))[:2]
    other1 = shifted(context1, "z_hi", 1)
    both0 = to_all(jnp.stack([context[0], other0]), "x")
    mass1 = share0 + (1.0 - shifted(share0, REP, 1))

    output0, sums0 = call(
        first_forward, [SMEM, FEATURES, wts, layer(0, (width, TOK)), layer(0, (width, TOK)), col],
        [out, sums], [shape((width, TOK), F32), shape((8, 8, TOK), F32)], flops,
        place, both0, weight, res, tgt, gain,
    )
    totals0 = lax.all_to_all(sums0, TP, 0, 0)
    both0, other1, share1 = lax.optimization_barrier((both0, other1, share1, sums0))[:3]
    both1 = to_all(jnp.stack([context1, other1]), "x")
    prev = shifted(both0, REP, 1)
    mass_in = shifted((1.0 - share1) * mass1, REP, 2)
    kept0, sent0 = call(
        first_backward, [sums, out, layer(0, (width, TOK)), col, row], [pair] * 2,
        [shape((width, TOK), BF16)] * 2, 20 * width * TOK,
        totals0, output0, tgt, gain, share0, steps=1,
    )
    recv0 = shifted(sent0, REP, 1)
    mass2 = share1 * mass1 + mass_in
    mass_later = shifted(after(mass2, sent0), REP, -2)

    output1, sums1 = call(
        second_forward,
        [SMEM, FEATURES, FEATURES, FEATURES, pair, pair, wts]
        + [layer(1, (width, TOK)), layer(1, (width, TOK)), col, row],
        [out, sums], [shape((width, TOK), F32), shape((8, 8, TOK), F32)], 3 * flops,
        place, both0, prev, both1, kept0, recv0, weight, res, tgt, gain, mass1,
    )
    totals1 = lax.all_to_all(sums1, TP, 0, 0)
    late = lax.optimization_barrier((both0, prev, kept0, recv0, sums1))[:4]
    (rows,) = call(
        first_rows, [SMEM, FEATURES, FEATURES, pair, pair], [rows_spec],
        [shape((8, CHUNK, width), F32)], 2 * flops, place, *late,
    )
    coef = (share1 / mass2 + (1.0 - share1) / mass_later) / lax.axis_size(REP)
    kept, sent = call(
        second_backward, [SMEM, sums, out, layer(1, (width, TOK)), col, row, FEATURES, rows_spec],
        [cut] * 2, [shape((4, 8, 32, width), F32), shape((4, 8, 32, width), BF16)], flops,
        place, totals1, output1, tgt, gain, coef, both1, rows,
        scratch=[pltpu.VMEM((width, TOK), BF16), pltpu.VMEM((CHUNK, width), F32)],
    )

    total = (kept + shifted(sent, "core", 1).astype(F32)).astype(BF16)
    parts = lax.all_to_all(total, "y", 0, 0)
    total = jnp.sum(parts.astype(F32), axis=0).astype(BF16)
    parts = lax.all_to_all(total, "z_lo", 0, 0)
    gradient = jnp.sum(parts.astype(F32), axis=0)

    anchor_rows = lax.dynamic_slice_in_dim(slow_weight, lax.axis_index(REP) * 32, 32, 0)
    new_momentum = BETA * momentum + gradient
    new_weight = anchor_rows.astype(F32) - ALPHA * LR * new_momentum
    return (new_weight, new_momentum, mass2[0, :1])


def solution(mesh):
    fine = Mesh(mesh.devices.reshape(SIZES), AXES)
    return jax.shard_map(
        body,
        mesh=fine,
        in_specs=(
            P(None, REP, TP),
            P(None, REP, TP),
            P(None, REP, TP),
            P(TP),
            P(None, TP),
            P(REP, TP),
            P(None, REP),
        ),
        out_specs=(P(REP, TP), P(REP, TP), P(REP)),
        check_vma=False,
    )
```

```python
import jax
import jax.numpy as jnp
from jax import lax
from jax.sharding import Mesh, PartitionSpec as P

D = 2304
TOK = 512
LR = 0.005
BETA = 0.7
ALPHA = 1.0
EPS = 1e-06
SCALE = TOK ** (-0.5)

AXES = ("z_lo", "y", "core", "x", "z_hi")
SIZES = (8, 4, 2, 4, 2)
REP = AXES[:3]
TP = AXES[3:]
F32 = jnp.float32
BF16 = jnp.bfloat16


def shifted(value, axis, steps):
    count = lax.axis_size(axis)
    return lax.ppermute(value, axis, [(i, (i + steps) % count) for i in range(count)])


def after(value, *others):
    return lax.optimization_barrier((value,) + others)[0]


def to_all(value, axis):
    count = lax.axis_size(axis)
    return lax.all_to_all(jnp.broadcast_to(value[None], (count,) + value.shape), axis, 0, 0)


def contract_rows(left, right):
    return lax.dot_general(left, right, (((0,), (0,)), ((), ())), preferred_element_type=F32)


def ordered(both, hi):
    low = jnp.where(hi == 0, both[:, 0], both[:, 1])
    high = jnp.where(hi == 0, both[:, 1], both[:, 0])
    both = jnp.stack([low, high], axis=1)
    return jnp.transpose(both, (2, 0, 1, 3)).reshape(TOK, 2048)


def from_others(value, x):
    blocks = jnp.stack([value] + [shifted(value, "x", k) for k in (1, 2, 3)])
    twice = jnp.concatenate([blocks[::-1], blocks[::-1]])
    return lax.dynamic_slice_in_dim(twice, 3 - x, 4, 0)


def coefficients(shares):
    first, second = shares
    mass1 = first + (1.0 - jnp.roll(first, 1))
    mass2 = second * mass1 + jnp.roll((1.0 - second) * mass1, 2)
    part = (second / mass2 + (1.0 - second) / jnp.roll(mass2, -2)) / first.shape[0]
    early = part * first + jnp.roll(part, -1) * (1.0 - first)
    return jnp.stack([mass1, mass2, part, early])


def forward(gathered, quotient, residual, targets, gain):
    output = residual.astype(F32) + jnp.dot(gathered, quotient, preferred_element_type=F32)
    scaled = gain * output
    sums = jnp.stack(
        [
            jnp.sum(output * output, axis=1),
            jnp.sum(scaled * scaled, axis=1),
            jnp.sum(scaled * targets.astype(F32), axis=1),
        ]
    )
    return output, sums


def backward(output, totals, targets, gain):
    root_sq = totals[0] / D + EPS
    root = jnp.sqrt(root_sq)
    projection = SCALE * (totals[1] / root_sq - totals[2] / root) / D
    normed = output / root[:, None]
    normed_grad = SCALE * gain * (gain * normed - targets.astype(F32))
    return ((normed_grad - normed * projection[:, None]) / root[:, None]).astype(BF16)


def body(context, residual, targets, gain, slow_weight, momentum, shares):
    hi = lax.axis_index("z_hi")
    core = lax.axis_index("core")
    anchor = slow_weight.astype(F32)

    other0 = shifted(context[0], "z_hi", 1)
    row = jnp.repeat(shares[:, 0], 64)[None]
    all_shares = to_all(row, REP)[:, 0]
    other0, all_shares = lax.optimization_barrier((other0, all_shares))
    context1 = after(context[1], other0)
    other1 = shifted(context1, "z_hi", 1)
    both0 = to_all(jnp.stack([context[0], other0]), "x")
    replica = lax.axis_index(REP)
    table = coefficients((all_shares[:, 0], all_shares[:, 64]))
    mine = lax.dynamic_slice_in_dim(table, replica, 1, 1)
    mine = after(mine, other1)
    share0 = shares[0, 0]
    gathered0 = ordered(both0, hi)

    output0, sums0 = forward(gathered0, slow_weight, residual[0], targets[0], gain)
    totals0 = jnp.sum(to_all(sums0, TP), axis=0)
    pair1 = jnp.stack([context1, other1])
    both1 = from_others(after(pair1, sums0), lax.axis_index("x"))
    gathered1 = ordered(both1, hi)
    grad0 = backward(output0, totals0, targets[0], gain)
    weight_grad0 = contract_rows(gathered0, grad0)

    incoming = shifted(((1.0 - share0) * weight_grad0).astype(BF16), REP, 1)
    step0 = share0 * weight_grad0 + incoming.astype(F32)
    quotient1 = (anchor - (LR / mine[0, 0]) * step0).astype(BF16)
    output1, sums1 = forward(gathered1, quotient1, residual[1], targets[1], gain)
    totals1 = jnp.sum(to_all(sums1, TP), axis=0)
    grad1 = backward(output1, totals1, targets[1], gain)
    weight_grad1 = contract_rows(gathered1, grad1)
    total = mine[3, 0] * weight_grad0 + mine[2, 0] * weight_grad1

    width = total.shape[1]
    total = total.reshape(8, 4, 2, 32, width)
    kept = jnp.where(core == 0, total[:, :, 0], total[:, :, 1])
    sent = jnp.where(core == 0, total[:, :, 1], total[:, :, 0]).astype(BF16)
    total = kept + shifted(sent, "core", 1).astype(F32)
    parts = jnp.transpose(total.astype(BF16), (1, 0, 2, 3))
    parts = lax.all_to_all(parts, "y", 0, 0)
    total = jnp.sum(parts.astype(F32), axis=0)
    parts = lax.all_to_all(total.astype(BF16), "z_lo", 0, 0)
    gradient = jnp.sum(parts.astype(F32), axis=0)

    anchor_rows = lax.dynamic_slice_in_dim(slow_weight, lax.axis_index(REP) * 32, 32, 0)
    new_momentum = BETA * momentum + gradient
    new_weight = anchor_rows.astype(F32) - ALPHA * LR * new_momentum
    return (new_weight, new_momentum, mine[1])


def solution(mesh):
    fine = Mesh(mesh.devices.reshape(SIZES), AXES)
    return jax.shard_map(
        body,
        mesh=fine,
        in_specs=(
            P(None, REP, TP),
            P(None, REP, TP),
            P(None, REP, TP),
            P(TP),
            P(None, TP),
            P(REP, TP),
            P(None, REP),
        ),
        out_specs=(P(REP, TP), P(REP, TP), P(REP)),
        check_vma=False,
    )
```

```python
import jax
import jax.numpy as jnp
from jax import lax
from jax.sharding import Mesh, PartitionSpec as P

D = 2304
TOK = 512
LR = 0.005
BETA = 0.7
ALPHA = 1.0
EPS = 1e-06
SCALE = TOK ** (-0.5)

AXES = ("z_lo", "y", "core", "x", "z_hi")
SIZES = (8, 4, 2, 4, 2)
REP = AXES[:3]
TP = AXES[3:]
F32 = jnp.float32
BF16 = jnp.bfloat16


def shifted(value, axis, steps):
    count = lax.axis_size(axis)
    return lax.ppermute(value, axis, [(i, (i + steps) % count) for i in range(count)])


def after(value, *others):
    return lax.optimization_barrier((value,) + others)[0]


def to_all(value, axis):
    count = lax.axis_size(axis)
    return lax.all_to_all(jnp.broadcast_to(value[None], (count,) + value.shape), axis, 0, 0)


def contract_rows(left, right):
    return lax.dot_general(left, right, (((0,), (0,)), ((), ())), preferred_element_type=F32)


def ordered(both, hi):
    low = jnp.where(hi == 0, both[:, 0], both[:, 1])
    high = jnp.where(hi == 0, both[:, 1], both[:, 0])
    both = jnp.stack([low, high], axis=1)
    return jnp.transpose(both, (2, 0, 1, 3)).reshape(TOK, 2048)


def from_others(value, x):
    blocks = jnp.stack([value] + [shifted(value, "x", k) for k in (1, 2, 3)])
    twice = jnp.concatenate([blocks[::-1], blocks[::-1]])
    return lax.dynamic_slice_in_dim(twice, 3 - x, 4, 0)


def merged(own, other, hi):
    low = jnp.where(hi == 0, own, other)
    high = jnp.where(hi == 0, other, own)
    both = jnp.stack([low, high], axis=1)
    return jnp.transpose(both, (2, 0, 1, 3)).reshape(TOK, 2048)


def forward(gathered, quotient, residual, targets, gain):
    output = residual.astype(F32) + jnp.dot(gathered, quotient, preferred_element_type=F32)
    scaled = gain * output
    sums = jnp.stack(
        [
            jnp.sum(output * output, axis=1),
            jnp.sum(scaled * scaled, axis=1),
            jnp.sum(scaled * targets.astype(F32), axis=1),
        ]
    )
    return output, sums


def backward(output, totals, targets, gain):
    root_sq = totals[0] / D + EPS
    root = jnp.sqrt(root_sq)
    projection = SCALE * (totals[1] / root_sq - totals[2] / root) / D
    normed = output / root[:, None]
    normed_grad = SCALE * gain * (gain * normed - targets.astype(F32))
    return ((normed_grad - normed * projection[:, None]) / root[:, None]).astype(BF16)


def body(context, residual, targets, gain, slow_weight, momentum, shares):
    x, hi, core = lax.axis_index("x"), lax.axis_index("z_hi"), lax.axis_index("core")
    anchor = slow_weight.astype(F32)

    other0 = shifted(context[0], "z_hi", 1)
    before0 = shifted(shares[0], REP, 1)
    own0 = from_others(context[0], x)
    mass1 = shares[0] + (1.0 - before0)
    other0, own0, mass1 = lax.optimization_barrier((other0, own0, mass1))
    wide0 = to_all(other0, "x")
    context1 = after(context[1], other0)
    other1 = shifted(context1, "z_hi", 1)
    mass_in = shifted((1.0 - shares[1]) * mass1, REP, 2)
    own0, wide0, mass_in = lax.optimization_barrier((own0, wide0, mass_in))
    gathered0 = merged(own0, wide0, hi)
    mass2 = shares[1] * mass1 + mass_in
    share0 = shares[0, 0]

    output0, sums0 = forward(gathered0, slow_weight, residual[0], targets[0], gain)
    totals0 = jnp.sum(to_all(sums0, TP), axis=0)
    pair1 = jnp.stack([context1, other1])
    both1 = from_others(after(pair1, sums0), x)
    gathered1 = ordered(both1, hi)
    grad0 = backward(output0, totals0, targets[0], gain)
    weight_grad0 = contract_rows(gathered0, grad0)

    incoming = shifted(((1.0 - share0) * weight_grad0).astype(BF16), REP, 1)
    mass_later = shifted(after(mass2, weight_grad0), REP, -2)
    step0 = share0 * weight_grad0 + incoming.astype(F32)
    quotient1 = (anchor - (LR / mass1[0]) * step0).astype(BF16)
    output1, sums1 = forward(gathered1, quotient1, residual[1], targets[1], gain)
    totals1 = jnp.sum(to_all(sums1, TP), axis=0)
    grad1 = backward(output1, totals1, targets[1], gain)
    weight_grad1 = contract_rows(gathered1, grad1)
    part = (shares[1] / mass2 + (1.0 - shares[1]) / mass_later) / lax.axis_size(REP)
    total = part[0] * (step0 + weight_grad1)

    width = total.shape[1]
    total = total.reshape(8, 4, 2, 32, width)
    kept = jnp.where(core == 0, total[:, :, 0], total[:, :, 1])
    sent = jnp.where(core == 0, total[:, :, 1], total[:, :, 0]).astype(BF16)
    total = kept + shifted(sent, "core", 1).astype(F32)
    parts = jnp.transpose(total.astype(BF16), (1, 0, 2, 3))
    parts = lax.all_to_all(parts, "y", 0, 0)
    total = jnp.sum(parts.astype(F32), axis=0)
    parts = lax.all_to_all(total.astype(BF16), "z_lo", 0, 0)
    gradient = jnp.sum(parts.astype(F32), axis=0)

    anchor_rows = lax.dynamic_slice_in_dim(slow_weight, lax.axis_index(REP) * 32, 32, 0)
    new_momentum = BETA * momentum + gradient
    new_weight = anchor_rows.astype(F32) - ALPHA * LR * new_momentum
    return (new_weight, new_momentum, mass2)


def solution(mesh):
    fine = Mesh(mesh.devices.reshape(SIZES), AXES)
    return jax.shard_map(
        body,
        mesh=fine,
        in_specs=(
            P(None, REP, TP),
            P(None, REP, TP),
            P(None, REP, TP),
            P(TP),
            P(None, TP),
            P(REP, TP),
            P(None, REP),
        ),
        out_specs=(P(REP, TP), P(REP, TP), P(REP)),
        check_vma=False,
    )
```

```python
import jax
import jax.numpy as jnp
from jax import lax
from jax.sharding import Mesh, PartitionSpec as P

D = 2304
TOK = 512
LR = 0.005
BETA = 0.7
ALPHA = 1.0
EPS = 1e-06
SCALE = TOK ** (-0.5)

AXES = ("z_lo", "y", "core", "x", "z_hi")
SIZES = (8, 4, 2, 4, 2)
REP = AXES[:3]
TP = AXES[3:]
F32 = jnp.float32
BF16 = jnp.bfloat16


def shifted(value, axis, steps):
    count = lax.axis_size(axis)
    return lax.ppermute(value, axis, [(i, (i + steps) % count) for i in range(count)])


def after(value, *others):
    return lax.optimization_barrier((value,) + others)[0]


def to_all(value, axis):
    count = lax.axis_size(axis)
    return lax.all_to_all(jnp.broadcast_to(value[None], (count,) + value.shape), axis, 0, 0)


def contract_rows(left, right):
    return lax.dot_general(left, right, (((0,), (0,)), ((), ())), preferred_element_type=F32)


def ordered(both, hi):
    low = jnp.where(hi == 0, both[:, 0], both[:, 1])
    high = jnp.where(hi == 0, both[:, 1], both[:, 0])
    both = jnp.stack([low, high], axis=1)
    return jnp.transpose(both, (2, 0, 1, 3)).reshape(TOK, 2048)


def along_x(value):
    return [value] + [shifted(value, "x", k) for k in (1, 2, 3)]


def in_order(blocks, x):
    blocks = jnp.stack(blocks)
    twice = jnp.concatenate([blocks[::-1], blocks[::-1]])
    return lax.dynamic_slice_in_dim(twice, 3 - x, 4, 0)


def merged(own, other, hi):
    low = jnp.where(hi == 0, own, other)
    high = jnp.where(hi == 0, other, own)
    both = jnp.stack([low, high], axis=1)
    return jnp.transpose(both, (2, 0, 1, 3)).reshape(TOK, 2048)


def mass_neighbours(shares, before):
    near = {k: shifted(shares, REP, -k) for k in (-3, -2, 1, 2)}
    return {**near, -1: before, 0: shares}


def masses(near):
    mass1 = {k: near[k][0] + (1.0 - near[k - 1][0]) for k in (-2, 0, 2)}
    mass2 = {k: near[k][1] * mass1[k] + (1.0 - near[k - 2][1]) * mass1[k - 2] for k in (0, 2)}
    own = near[0][1]
    return mass2[0], (own / mass2[0] + (1.0 - own) / mass2[2]) / lax.axis_size(REP)


def forward(gathered, quotient, residual, targets, gain):
    output = residual.astype(F32) + jnp.dot(gathered, quotient, preferred_element_type=F32)
    scaled = gain * output
    sums = jnp.stack(
        [
            jnp.sum(output * output, axis=1),
            jnp.sum(scaled * scaled, axis=1),
            jnp.sum(scaled * targets.astype(F32), axis=1),
        ]
    )
    return output, sums


def backward(output, totals, targets, gain):
    root_sq = totals[0] / D + EPS
    root = jnp.sqrt(root_sq)
    projection = SCALE * (totals[1] / root_sq - totals[2] / root) / D
    normed = output / root[:, None]
    normed_grad = SCALE * gain * (gain * normed - targets.astype(F32))
    return ((normed_grad - normed * projection[:, None]) / root[:, None]).astype(BF16)


def body(context, residual, targets, gain, slow_weight, momentum, shares):
    x, hi, core = lax.axis_index("x"), lax.axis_index("z_hi"), lax.axis_index("core")
    anchor = slow_weight.astype(F32)

    other0 = shifted(context[0], "z_hi", 1)
    own0 = along_x(context[0])
    before = shifted(shares[:, 0], REP, 1)
    other0, own0, before = lax.optimization_barrier((other0, own0, before))
    wide0 = to_all(other0, "x")
    own0 = in_order(own0, x)
    context1 = after(context[1], other0)
    other1 = shifted(context1, "z_hi", 1)
    gathered0 = merged(own0, wide0, hi)
    share0 = shares[0, 0]

    output0, sums0 = forward(gathered0, slow_weight, residual[0], targets[0], gain)
    totals0 = jnp.sum(to_all(sums0, TP), axis=0)
    pair1 = jnp.stack([context1, other1])
    both1 = in_order(along_x(after(pair1, sums0)), x)
    gathered1 = ordered(both1, hi)
    grad0 = backward(output0, totals0, targets[0], gain)
    weight_grad0 = contract_rows(gathered0, grad0)

    pushed = ((1.0 - share0) * weight_grad0).astype(BF16)
    incoming = shifted(pushed, REP, 1)
    mass1 = share0 + (1.0 - before[0])
    step0 = share0 * weight_grad0 + incoming.astype(F32)
    quotient1 = (anchor - (LR / mass1) * step0).astype(BF16)
    output1, sums1 = forward(gathered1, quotient1, residual[1], targets[1], gain)
    near = mass_neighbours(shares[:, 0], before)
    near = lax.optimization_barrier((near, sums1))[0]
    mass2, part = masses(near)
    totals1 = jnp.sum(to_all(sums1, TP), axis=0)
    grad1 = backward(output1, totals1, targets[1], gain)
    weight_grad1 = contract_rows(gathered1, grad1)
    total = (part * (step0 + weight_grad1)).astype(BF16)

    width = total.shape[1]
    total = total.reshape(8, 4, 2, 32, width)
    kept = jnp.where(core == 0, total[:, :, 0], total[:, :, 1])
    sent = jnp.where(core == 0, total[:, :, 1], total[:, :, 0])
    total = kept.astype(F32) + shifted(sent, "core", 1).astype(F32)
    parts = jnp.transpose(total.astype(BF16), (1, 0, 2, 3))
    parts = lax.all_to_all(parts, "y", 0, 0)
    total = jnp.sum(parts.astype(F32), axis=0)
    parts = lax.all_to_all(total.astype(BF16), "z_lo", 0, 0)
    gradient = jnp.sum(parts.astype(F32), axis=0)

    anchor_rows = lax.dynamic_slice_in_dim(slow_weight, lax.axis_index(REP) * 32, 32, 0)
    new_momentum = BETA * momentum + gradient
    new_weight = anchor_rows.astype(F32) - ALPHA * LR * new_momentum
    return (new_weight, new_momentum, mass2[None])


def solution(mesh):
    fine = Mesh(mesh.devices.reshape(SIZES), AXES)
    return jax.shard_map(
        body,
        mesh=fine,
        in_specs=(
            P(None, REP, TP),
            P(None, REP, TP),
            P(None, REP, TP),
            P(TP),
            P(None, TP),
            P(REP, TP),
            P(None, REP),
        ),
        out_specs=(P(REP, TP), P(REP, TP), P(REP)),
        check_vma=False,
    )
```

```python
import jax
import jax.numpy as jnp
from jax import lax
from jax.sharding import Mesh, PartitionSpec as P

D = 2304
TOK = 512
LR = 0.005
BETA = 0.7
ALPHA = 1.0
EPS = 1e-06
SCALE = TOK ** (-0.5)

AXES = ("z_lo", "y", "core", "x", "z_hi")
SIZES = (8, 4, 2, 4, 2)
REP = AXES[:3]
TP = AXES[3:]
F32 = jnp.float32
BF16 = jnp.bfloat16


def shifted(value, axis, steps):
    count = lax.axis_size(axis)
    return lax.ppermute(value, axis, [(i, (i + steps) % count) for i in range(count)])


def after(value, *others):
    return lax.optimization_barrier((value,) + others)[0]


def to_all(value, axis):
    count = lax.axis_size(axis)
    return lax.all_to_all(jnp.broadcast_to(value[None], (count,) + value.shape), axis, 0, 0)


def contract_rows(left, right):
    return lax.dot_general(left, right, (((0,), (0,)), ((), ())), preferred_element_type=F32)


def ordered(both, hi):
    low = jnp.where(hi == 0, both[:, 0], both[:, 1])
    high = jnp.where(hi == 0, both[:, 1], both[:, 0])
    both = jnp.stack([low, high], axis=1)
    return jnp.transpose(both, (2, 0, 1, 3)).reshape(TOK, 2048)


def along_x(value):
    return [value] + [shifted(value, "x", k) for k in (1, 2, 3)]


def in_order(blocks, x):
    placed = jnp.broadcast_to(blocks[0][None], (4,) + blocks[0].shape)
    for k in (2, 1, 3):
        placed = lax.dynamic_update_slice_in_dim(placed, blocks[k][None], (x - k) & 3, 0)
    return placed


def by_half(own, other, hi):
    return jnp.where(hi == 0, jnp.stack([own, other]), jnp.stack([other, own]))


def laid_out(blocks):
    return jnp.transpose(blocks, (2, 0, 1, 3)).reshape(TOK, 2048)


def forward(gathered, quotient, residual, targets, gain):
    output = residual.astype(F32) + jnp.dot(gathered, quotient, preferred_element_type=F32)
    scaled = gain * output
    sums = jnp.stack(
        [
            jnp.sum(output * output, axis=1),
            jnp.sum(scaled * scaled, axis=1),
            jnp.sum(scaled * targets.astype(F32), axis=1),
        ]
    )
    return output, sums


def backward(output, totals, targets, gain):
    root_sq = totals[0] / D + EPS
    root = jnp.sqrt(root_sq)
    projection = SCALE * (totals[1] / root_sq - totals[2] / root) / D
    normed = output / root[:, None]
    normed_grad = SCALE * gain * (gain * normed - targets.astype(F32))
    return ((normed_grad - normed * projection[:, None]) / root[:, None]).astype(BF16)


def body(context, residual, targets, gain, slow_weight, momentum, shares):
    x, hi, core = lax.axis_index("x"), lax.axis_index("z_hi"), lax.axis_index("core")
    anchor = slow_weight.astype(F32)

    other0 = shifted(context[0], "z_hi", 1)
    own0 = along_x(context[0])
    before = shifted(shares[0], REP, 1)
    other0, own0, before = lax.optimization_barrier((other0, own0, before))
    wide0 = to_all(other0, "x")
    own0 = in_order(own0, x)
    context1 = after(context[1], other0)
    other1 = shifted(context1, "z_hi", 1)
    gathered0 = laid_out(jnp.where(hi == 0, jnp.stack([own0, wide0], 1), jnp.stack([wide0, own0], 1)))
    share0 = shares[0, 0]

    output0, sums0 = forward(gathered0, slow_weight, residual[0], targets[0], gain)
    totals0 = jnp.sum(to_all(sums0, TP), axis=0)
    pair1 = by_half(context1, other1, hi)
    both1 = in_order(along_x(after(pair1, sums0)), x)
    gathered1 = laid_out(both1)
    grad0 = backward(output0, totals0, targets[0], gain)
    weight_grad0 = contract_rows(gathered0, grad0)

    pushed = ((1.0 - share0) * weight_grad0).astype(BF16)
    incoming = shifted(pushed, REP, 1)
    mass_in = shifted((1.0 - shares[1]) * (shares[0] + (1.0 - before)), REP, 2)
    incoming, mass_in = lax.optimization_barrier((incoming, mass_in))
    mass1 = share0 + (1.0 - before[0])
    step0 = share0 * weight_grad0 + incoming.astype(F32)
    quotient1 = (anchor - (LR / mass1) * step0).astype(BF16)
    output1, sums1 = forward(gathered1, quotient1, residual[1], targets[1], gain)
    mass2 = shares[1] * (shares[0] + (1.0 - before)) + mass_in
    mass_later = shifted(mass2, REP, -2)
    part = ((shares[1] / mass2 + (1.0 - shares[1]) / mass_later) / lax.axis_size(REP))[0]
    totals1 = jnp.sum(to_all(sums1, TP), axis=0)
    grad1 = backward(output1, totals1, targets[1], gain)
    weight_grad1 = contract_rows(gathered1, grad1)
    total = (part * (step0 + weight_grad1)).astype(BF16)

    width = total.shape[1]
    total = total.reshape(8, 4, 2, 32, width)
    kept = jnp.where(core == 0, total[:, :, 0], total[:, :, 1])
    sent = jnp.where(core == 0, total[:, :, 1], total[:, :, 0])
    total = kept.astype(F32) + shifted(sent, "core", 1).astype(F32)
    parts = jnp.transpose(total.astype(BF16), (1, 0, 2, 3))
    parts = lax.all_to_all(parts, "y", 0, 0)
    total = jnp.sum(parts.astype(F32), axis=0)
    parts = lax.all_to_all(total.astype(BF16), "z_lo", 0, 0)
    gradient = jnp.sum(parts.astype(F32), axis=0)

    anchor_rows = lax.dynamic_slice_in_dim(slow_weight, lax.axis_index(REP) * 32, 32, 0)
    new_momentum = BETA * momentum + gradient
    new_weight = anchor_rows.astype(F32) - ALPHA * LR * new_momentum
    return (new_weight, new_momentum, mass2)


def solution(mesh):
    fine = Mesh(mesh.devices.reshape(SIZES), AXES)
    return jax.shard_map(
        body,
        mesh=fine,
        in_specs=(
            P(None, REP, TP),
            P(None, REP, TP),
            P(None, REP, TP),
            P(TP),
            P(None, TP),
            P(REP, TP),
            P(None, REP),
        ),
        out_specs=(P(REP, TP), P(REP, TP), P(REP)),
        check_vma=False,
    )
```

```python
import jax
import jax.numpy as jnp
from jax import lax
from jax.sharding import Mesh, PartitionSpec as P

D = 2304
TOK = 512
LR = 0.005
BETA = 0.7
ALPHA = 1.0
EPS = 1e-06
SCALE = TOK ** (-0.5)

AXES = ("z_lo", "y", "core", "x", "z_hi")
SIZES = (8, 4, 2, 4, 2)
REP = AXES[:3]
TP = AXES[3:]
F32 = jnp.float32
BF16 = jnp.bfloat16


def shifted(value, axis, steps):
    count = lax.axis_size(axis)
    return lax.ppermute(value, axis, [(i, (i + steps) % count) for i in range(count)])


def after(value, *others):
    return lax.optimization_barrier((value,) + others)[0]


def to_all(value, axis):
    count = lax.axis_size(axis)
    return lax.all_to_all(jnp.broadcast_to(value[None], (count,) + value.shape), axis, 0, 0)


def contract_rows(left, right):
    return lax.dot_general(left, right, (((0,), (0,)), ((), ())), preferred_element_type=F32)


def ordered(both, hi):
    low = jnp.where(hi == 0, both[:, 0], both[:, 1])
    high = jnp.where(hi == 0, both[:, 1], both[:, 0])
    both = jnp.stack([low, high], axis=1)
    return jnp.transpose(both, (2, 0, 1, 3)).reshape(TOK, 2048)


def along_x(value):
    return [value] + [shifted(value, "x", k) for k in (1, 2, 3)]


def in_order(blocks, x):
    placed = jnp.broadcast_to(blocks[0][None], (4,) + blocks[0].shape)
    for k in (2, 1, 3):
        placed = lax.dynamic_update_slice_in_dim(placed, blocks[k][None], (x - k) & 3, 0)
    return placed


def by_half(own, other, hi):
    return jnp.where(hi == 0, jnp.stack([own, other]), jnp.stack([other, own]))


def laid_out(blocks):
    return jnp.transpose(blocks, (2, 0, 1, 3)).reshape(TOK, 2048)


def forward(gathered, quotient, residual, targets, gain):
    output = residual.astype(F32) + jnp.dot(gathered, quotient, preferred_element_type=F32)
    scaled = gain * output
    sums = jnp.stack(
        [
            jnp.sum(output * output, axis=1),
            jnp.sum(scaled * scaled, axis=1),
            jnp.sum(scaled * targets.astype(F32), axis=1),
        ]
    )
    return output, sums


def backward(output, totals, targets, gain):
    root_sq = totals[0] / D + EPS
    root = jnp.sqrt(root_sq)
    projection = SCALE * (totals[1] / root_sq - totals[2] / root) / D
    normed = output / root[:, None]
    normed_grad = SCALE * gain * (gain * normed - targets.astype(F32))
    return ((normed_grad - normed * projection[:, None]) / root[:, None]).astype(BF16)


def body(context, residual, targets, gain, slow_weight, momentum, shares):
    x, hi, core = lax.axis_index("x"), lax.axis_index("z_hi"), lax.axis_index("core")
    anchor = slow_weight.astype(F32)

    other0 = shifted(context[0], "z_hi", 1)
    own0 = along_x(context[0])
    before = shifted(shares[0], REP, 1)
    mass1 = shares[0] + (1.0 - before)
    leaving = (1.0 - shares[1]) * mass1
    other0, own0, mass1, leaving = lax.optimization_barrier((other0, own0, mass1, leaving))
    wide0 = to_all(other0, "x")
    own0 = in_order(own0, x)
    context1 = after(context[1], other0)
    other1 = shifted(context1, "z_hi", 1)
    gathered0 = laid_out(jnp.where(hi == 0, jnp.stack([own0, wide0], 1), jnp.stack([wide0, own0], 1)))
    share0 = shares[0, 0]

    output0, sums0 = forward(gathered0, slow_weight, residual[0], targets[0], gain)
    totals0 = jnp.sum(to_all(sums0, TP), axis=0)
    pair1 = by_half(context1, other1, hi)
    both1 = in_order(lax.optimization_barrier(along_x(after(pair1, sums0))), x)
    gathered1 = laid_out(both1)
    grad0 = backward(output0, totals0, targets[0], gain)
    weight_grad0 = contract_rows(gathered0, grad0)

    pushed = ((1.0 - share0) * weight_grad0).astype(BF16)
    incoming = shifted(pushed, REP, 1)
    mass_in = shifted(leaving, REP, 2)
    incoming, mass_in = lax.optimization_barrier((incoming, mass_in))
    step0 = share0 * weight_grad0 + incoming.astype(F32)
    quotient1 = (anchor - (LR / mass1[0]) * step0).astype(BF16)
    output1, sums1 = forward(gathered1, quotient1, residual[1], targets[1], gain)
    mass2 = shares[1] * mass1 + mass_in
    mass_later = shifted(mass2, REP, -2)
    part = ((shares[1] / mass2 + (1.0 - shares[1]) / mass_later) / lax.axis_size(REP))[0]
    totals1 = jnp.sum(to_all(sums1, TP), axis=0)
    grad1 = backward(output1, totals1, targets[1], gain)
    weight_grad1 = contract_rows(gathered1, grad1)
    total = (part * (step0 + weight_grad1)).astype(BF16)

    width = total.shape[1]
    total = total.reshape(8, 4, 2, 32, width)
    kept = jnp.where(core == 0, total[:, :, 0], total[:, :, 1])
    sent = jnp.where(core == 0, total[:, :, 1], total[:, :, 0])
    total = kept.astype(F32) + shifted(sent, "core", 1).astype(F32)
    parts = jnp.transpose(total.astype(BF16), (1, 0, 2, 3))
    parts = lax.all_to_all(parts, "y", 0, 0)
    total = jnp.sum(parts.astype(F32), axis=0)
    parts = lax.all_to_all(total.astype(BF16), "z_lo", 0, 0)
    gradient = jnp.sum(parts.astype(F32), axis=0)

    anchor_rows = lax.dynamic_slice_in_dim(slow_weight, lax.axis_index(REP) * 32, 32, 0)
    new_momentum = BETA * momentum + gradient
    new_weight = anchor_rows.astype(F32) - ALPHA * LR * new_momentum
    return (new_weight, new_momentum, mass2)


def solution(mesh):
    fine = Mesh(mesh.devices.reshape(SIZES), AXES)
    return jax.shard_map(
        body,
        mesh=fine,
        in_specs=(
            P(None, REP, TP),
            P(None, REP, TP),
            P(None, REP, TP),
            P(TP),
            P(None, TP),
            P(REP, TP),
            P(None, REP),
        ),
        out_specs=(P(REP, TP), P(REP, TP), P(REP)),
        check_vma=False,
    )
```

```python
import jax
import jax.numpy as jnp
from jax import lax
from jax.sharding import Mesh, PartitionSpec as P

D = 2304
TOK = 512
LR = 0.005
BETA = 0.7
ALPHA = 1.0
EPS = 1e-06
SCALE = TOK ** (-0.5)

AXES = ("z_lo", "y", "core", "x", "z_hi")
SIZES = (8, 4, 2, 4, 2)
REP = AXES[:3]
TP = AXES[3:]
F32 = jnp.float32
BF16 = jnp.bfloat16


def shifted(value, axis, steps):
    count = lax.axis_size(axis)
    return lax.ppermute(value, axis, [(i, (i + steps) % count) for i in range(count)])


def after(value, *others):
    return lax.optimization_barrier((value,) + others)[0]


def to_all(value, axis):
    count = lax.axis_size(axis)
    return lax.all_to_all(jnp.broadcast_to(value[None], (count,) + value.shape), axis, 0, 0)


def contract_rows(left, right):
    return lax.dot_general(left, right, (((0,), (0,)), ((), ())), preferred_element_type=F32)


def ordered(both, hi):
    low = jnp.where(hi == 0, both[:, 0], both[:, 1])
    high = jnp.where(hi == 0, both[:, 1], both[:, 0])
    both = jnp.stack([low, high], axis=1)
    return jnp.transpose(both, (2, 0, 1, 3)).reshape(TOK, 2048)


def along_x(value):
    return [value] + [shifted(value, "x", k) for k in (1, 2, 3)]


def in_order(blocks, x):
    placed = jnp.broadcast_to(blocks[0][None], (4,) + blocks[0].shape)
    for k in (2, 1, 3):
        placed = lax.dynamic_update_slice_in_dim(placed, blocks[k][None], (x - k) & 3, 0)
    return placed


def by_half(own, other, hi):
    return jnp.where(hi == 0, jnp.stack([own, other]), jnp.stack([other, own]))


def laid_out(blocks):
    return jnp.transpose(blocks, (2, 0, 1, 3)).reshape(TOK, 2048)


def mass_neighbours(shares, before):
    near = {k: shifted(shares, REP, -k) for k in (-3, -2, 1, 2)}
    return {**near, -1: before, 0: shares}


def masses(near):
    mass1 = {k: near[k][0] + (1.0 - near[k - 1][0]) for k in (-2, 0, 2)}
    mass2 = {k: near[k][1] * mass1[k] + (1.0 - near[k - 2][1]) * mass1[k - 2] for k in (0, 2)}
    own = near[0][1]
    return mass2[0], (own / mass2[0] + (1.0 - own) / mass2[2]) / lax.axis_size(REP)


def forward(gathered, quotient, residual, targets, gain):
    output = residual.astype(F32) + jnp.dot(gathered, quotient, preferred_element_type=F32)
    scaled = gain * output
    sums = jnp.stack(
        [
            jnp.sum(output * output, axis=1),
            jnp.sum(scaled * scaled, axis=1),
            jnp.sum(scaled * targets.astype(F32), axis=1),
        ]
    )
    return output, sums


def backward(output, totals, targets, gain):
    root_sq = totals[0] / D + EPS
    root = jnp.sqrt(root_sq)
    projection = SCALE * (totals[1] / root_sq - totals[2] / root) / D
    normed = output / root[:, None]
    normed_grad = SCALE * gain * (gain * normed - targets.astype(F32))
    return ((normed_grad - normed * projection[:, None]) / root[:, None]).astype(BF16)


def body(context, residual, targets, gain, slow_weight, momentum, shares):
    x, hi, core = lax.axis_index("x"), lax.axis_index("z_hi"), lax.axis_index("core")
    anchor = slow_weight.astype(F32)

    other0 = shifted(context[0], "z_hi", 1)
    own0 = along_x(context[0])
    other0, own0, late_shares = lax.optimization_barrier((other0, own0, shares))
    before = shifted(late_shares[:, 0], REP, 1)
    wide0, before = lax.optimization_barrier((to_all(other0, "x"), before))
    own0 = in_order(own0, x)
    mass1 = shares[0, 0] + (1.0 - before[0])
    context1 = after(context[1], other0)
    other1 = shifted(context1, "z_hi", 1)
    gathered0 = laid_out(jnp.where(hi == 0, jnp.stack([own0, wide0], 1), jnp.stack([wide0, own0], 1)))
    share0 = shares[0, 0]

    output0, sums0 = forward(gathered0, slow_weight, residual[0], targets[0], gain)
    totals0 = jnp.sum(to_all(sums0, TP), axis=0)
    pair1 = by_half(context1, other1, hi)
    both1 = in_order(lax.optimization_barrier(along_x(after(pair1, sums0))), x)
    gathered1 = laid_out(both1)
    grad0 = backward(output0, totals0, targets[0], gain)
    weight_grad0 = contract_rows(gathered0, grad0)

    pushed = ((1.0 - share0) * weight_grad0).astype(BF16)
    incoming = shifted(pushed, REP, 1)
    step0 = share0 * weight_grad0 + incoming.astype(F32)
    quotient1 = (anchor - (LR / mass1) * step0).astype(BF16)
    output1, sums1 = forward(gathered1, quotient1, residual[1], targets[1], gain)
    near = mass_neighbours(shares[:, 0], before)
    near = lax.optimization_barrier((near, sums1))[0]
    mass2, part = masses(near)
    totals1 = jnp.sum(to_all(sums1, TP), axis=0)
    grad1 = backward(output1, totals1, targets[1], gain)
    weight_grad1 = contract_rows(gathered1, grad1)
    total = (part * (step0 + weight_grad1)).astype(BF16)

    width = total.shape[1]
    total = total.reshape(8, 4, 2, 32, width)
    kept = jnp.where(core == 0, total[:, :, 0], total[:, :, 1])
    sent = jnp.where(core == 0, total[:, :, 1], total[:, :, 0])
    total = kept.astype(F32) + shifted(sent, "core", 1).astype(F32)
    parts = jnp.transpose(total.astype(BF16), (1, 0, 2, 3))
    parts = lax.all_to_all(parts, "y", 0, 0)
    total = jnp.sum(parts.astype(F32), axis=0)
    parts = lax.all_to_all(total.astype(BF16), "z_lo", 0, 0)
    gradient = jnp.sum(parts.astype(F32), axis=0)

    anchor_rows = lax.dynamic_slice_in_dim(slow_weight, lax.axis_index(REP) * 32, 32, 0)
    new_momentum = BETA * momentum + gradient
    new_weight = anchor_rows.astype(F32) - ALPHA * LR * new_momentum
    return (new_weight, new_momentum, mass2[None])


def solution(mesh):
    fine = Mesh(mesh.devices.reshape(SIZES), AXES)
    return jax.shard_map(
        body,
        mesh=fine,
        in_specs=(
            P(None, REP, TP),
            P(None, REP, TP),
            P(None, REP, TP),
            P(TP),
            P(None, TP),
            P(REP, TP),
            P(None, REP),
        ),
        out_specs=(P(REP, TP), P(REP, TP), P(REP)),
        check_vma=False,
    )
```

```python
import jax
import jax.numpy as jnp
from jax import lax
from jax.sharding import Mesh, PartitionSpec as P

D = 2304
TOK = 512
LR = 0.005
BETA = 0.7
ALPHA = 1.0
EPS = 1e-06
SCALE = TOK ** (-0.5)

AXES = ("z_lo", "y", "core", "x", "z_hi")
SIZES = (8, 4, 2, 4, 2)
REP = AXES[:3]
TP = AXES[3:]
F32 = jnp.float32
BF16 = jnp.bfloat16


def shifted(value, axis, steps):
    count = lax.axis_size(axis)
    return lax.ppermute(value, axis, [(i, (i + steps) % count) for i in range(count)])


def after(value, *others):
    return lax.optimization_barrier((value,) + others)[0]


def to_all(value, axis):
    count = lax.axis_size(axis)
    return lax.all_to_all(jnp.broadcast_to(value[None], (count,) + value.shape), axis, 0, 0)


def contract_rows(left, right):
    return lax.dot_general(left, right, (((0,), (0,)), ((), ())), preferred_element_type=F32)


def ordered(both, hi):
    low = jnp.where(hi == 0, both[:, 0], both[:, 1])
    high = jnp.where(hi == 0, both[:, 1], both[:, 0])
    both = jnp.stack([low, high], axis=1)
    return jnp.transpose(both, (2, 0, 1, 3)).reshape(TOK, 2048)


def along_x(value):
    return [value] + [shifted(value, "x", k) for k in (1, 2, 3)]


def in_order(blocks, x, together=()):
    blocks = list(blocks)
    if together:
        waited = lax.optimization_barrier(tuple(blocks[k] for k in together))
        for k, block in zip(together, waited):
            blocks[k] = block
    placed = jnp.broadcast_to(blocks[0][None], (4,) + blocks[0].shape)
    for k in (2, 1, 3):
        placed = lax.dynamic_update_slice_in_dim(placed, blocks[k][None], (x - k) & 3, 0)
    return placed


def by_half(own, other, hi):
    return jnp.where(hi == 0, jnp.stack([own, other]), jnp.stack([other, own]))


def laid_out(blocks):
    return jnp.transpose(blocks, (2, 0, 1, 3)).reshape(TOK, 2048)


def forward(gathered, quotient, residual, targets, gain):
    output = residual.astype(F32) + jnp.dot(gathered, quotient, preferred_element_type=F32)
    scaled = gain * output
    sums = jnp.stack(
        [
            jnp.sum(output * output, axis=1),
            jnp.sum(scaled * scaled, axis=1),
            jnp.sum(scaled * targets.astype(F32), axis=1),
        ]
    )
    return output, sums


def backward(output, totals, targets, gain):
    root_sq = totals[0] / D + EPS
    root = jnp.sqrt(root_sq)
    projection = SCALE * (totals[1] / root_sq - totals[2] / root) / D
    normed = output / root[:, None]
    normed_grad = SCALE * gain * (gain * normed - targets.astype(F32))
    return ((normed_grad - normed * projection[:, None]) / root[:, None]).astype(BF16)


def body(context, residual, targets, gain, slow_weight, momentum, shares):
    x, hi, core = lax.axis_index("x"), lax.axis_index("z_hi"), lax.axis_index("core")
    anchor = slow_weight.astype(F32)

    other0 = shifted(context[0], "z_hi", 1)
    own0 = along_x(context[0])
    before = shifted(shares[0], REP, 1)
    mass1 = shares[0] + (1.0 - before)
    leaving = (1.0 - shares[1]) * mass1
    other0, own0, mass1, leaving = lax.optimization_barrier((other0, own0, mass1, leaving))
    wide0 = to_all(other0, "x")
    own0 = in_order(own0, x)
    context1 = after(context[1], other0)
    other1 = shifted(context1, "z_hi", 1)
    gathered0 = laid_out(jnp.where(hi == 0, jnp.stack([own0, wide0], 1), jnp.stack([wide0, own0], 1)))
    share0 = shares[0, 0]

    output0, sums0 = forward(gathered0, slow_weight, residual[0], targets[0], gain)
    totals0 = jnp.sum(to_all(sums0, TP), axis=0)
    pair1 = by_half(context1, other1, hi)
    both1 = in_order(along_x(after(pair1, sums0)), x, (1, 2))
    gathered1 = laid_out(both1)
    grad0 = backward(output0, totals0, targets[0], gain)
    weight_grad0 = contract_rows(gathered0, grad0)

    pushed = ((1.0 - share0) * weight_grad0).astype(BF16)
    incoming = shifted(pushed, REP, 1)
    mass_in = shifted(leaving, REP, 2)
    incoming, mass_in = lax.optimization_barrier((incoming, mass_in))
    step0 = share0 * weight_grad0 + incoming.astype(F32)
    quotient1 = (anchor - (LR / mass1[0]) * step0).astype(BF16)
    output1, sums1 = forward(gathered1, quotient1, residual[1], targets[1], gain)
    mass2 = shares[1] * mass1 + mass_in
    mass_later = shifted(mass2, REP, -2)
    part = ((shares[1] / mass2 + (1.0 - shares[1]) / mass_later) / lax.axis_size(REP))[0]
    totals1 = jnp.sum(to_all(sums1, TP), axis=0)
    grad1 = backward(output1, totals1, targets[1], gain)
    weight_grad1 = contract_rows(gathered1, grad1)
    total = (part * (step0 + weight_grad1)).astype(BF16)

    width = total.shape[1]
    total = total.reshape(8, 4, 2, 32, width)
    kept = jnp.where(core == 0, total[:, :, 0], total[:, :, 1])
    sent = jnp.where(core == 0, total[:, :, 1], total[:, :, 0])
    total = kept.astype(F32) + shifted(sent, "core", 1).astype(F32)
    parts = jnp.transpose(total.astype(BF16), (1, 0, 2, 3))
    parts = lax.all_to_all(parts, "y", 0, 0)
    total = jnp.sum(parts.astype(F32), axis=0)
    parts = lax.all_to_all(total.astype(BF16), "z_lo", 0, 0)
    gradient = jnp.sum(parts.astype(F32), axis=0)

    anchor_rows = lax.dynamic_slice_in_dim(slow_weight, lax.axis_index(REP) * 32, 32, 0)
    new_momentum = BETA * momentum + gradient
    new_weight = anchor_rows.astype(F32) - ALPHA * LR * new_momentum
    return (new_weight, new_momentum, mass2)


def solution(mesh):
    fine = Mesh(mesh.devices.reshape(SIZES), AXES)
    return jax.shard_map(
        body,
        mesh=fine,
        in_specs=(
            P(None, REP, TP),
            P(None, REP, TP),
            P(None, REP, TP),
            P(TP),
            P(None, TP),
            P(REP, TP),
            P(None, REP),
        ),
        out_specs=(P(REP, TP), P(REP, TP), P(REP)),
        check_vma=False,
    )
```

```python
import jax
import jax.numpy as jnp
from jax import lax
from jax.sharding import Mesh, PartitionSpec as P

D = 2304
TOK = 512
LR = 0.005
BETA = 0.7
ALPHA = 1.0
EPS = 1e-06
SCALE = TOK ** (-0.5)

AXES = ("z_lo", "y", "core", "x", "z_hi")
SIZES = (8, 4, 2, 4, 2)
REP = AXES[:3]
TP = AXES[3:]
F32 = jnp.float32
BF16 = jnp.bfloat16


def shifted(value, axis, steps):
    count = lax.axis_size(axis)
    return lax.ppermute(value, axis, [(i, (i + steps) % count) for i in range(count)])


def after(value, *others):
    return lax.optimization_barrier((value,) + others)[0]


def to_all(value, axis):
    count = lax.axis_size(axis)
    return lax.all_to_all(jnp.broadcast_to(value[None], (count,) + value.shape), axis, 0, 0)


def contract_rows(left, right):
    return lax.dot_general(left, right, (((0,), (0,)), ((), ())), preferred_element_type=F32)


def ordered(both, hi):
    low = jnp.where(hi == 0, both[:, 0], both[:, 1])
    high = jnp.where(hi == 0, both[:, 1], both[:, 0])
    both = jnp.stack([low, high], axis=1)
    return jnp.transpose(both, (2, 0, 1, 3)).reshape(TOK, 2048)


def along_x(value):
    return [value] + [shifted(value, "x", k) for k in (1, 2, 3)]


def in_order(blocks, x, together=()):
    blocks = list(blocks)
    if together:
        waited = lax.optimization_barrier(tuple(blocks[k] for k in together))
        for k, block in zip(together, waited):
            blocks[k] = block
    placed = jnp.broadcast_to(blocks[0][None], (4,) + blocks[0].shape)
    for k in (2, 1, 3):
        placed = lax.dynamic_update_slice_in_dim(placed, blocks[k][None], (x - k) & 3, 0)
    return placed


def by_half(own, other, hi):
    return jnp.where(hi == 0, jnp.stack([own, other]), jnp.stack([other, own]))


def laid_out(blocks):
    return jnp.transpose(blocks, (2, 0, 1, 3)).reshape(TOK, 2048)


def forward(gathered, quotient, residual, targets, gain):
    output = residual.astype(F32) + jnp.dot(gathered, quotient, preferred_element_type=F32)
    scaled = gain * output
    sums = jnp.stack(
        [
            jnp.sum(output * output, axis=1),
            jnp.sum(scaled * scaled, axis=1),
            jnp.sum(scaled * targets.astype(F32), axis=1),
        ]
    )
    return output, sums


def backward(output, totals, targets, gain):
    root_sq = totals[0] / D + EPS
    root = jnp.sqrt(root_sq)
    projection = SCALE * (totals[1] / root_sq - totals[2] / root) / D
    normed = output / root[:, None]
    normed_grad = SCALE * gain * (gain * normed - targets.astype(F32))
    return ((normed_grad - normed * projection[:, None]) / root[:, None]).astype(BF16)


def body(context, residual, targets, gain, slow_weight, momentum, shares):
    x, hi, core = lax.axis_index("x"), lax.axis_index("z_hi"), lax.axis_index("core")
    anchor = slow_weight.astype(F32)

    other0 = shifted(context[0], "z_hi", 1)
    own0 = along_x(context[0])
    before = shifted(shares[0], REP, 1)
    mass1 = shares[0] + (1.0 - before)
    leaving = (1.0 - shares[1]) * mass1
    other0, own0, mass1, leaving = lax.optimization_barrier((other0, own0, mass1, leaving))
    wide0 = to_all(other0, "x")
    own0 = in_order(own0, x)
    context1 = after(context[1], other0)
    other1 = shifted(context1, "z_hi", 1)
    gathered0 = laid_out(jnp.where(hi == 0, jnp.stack([own0, wide0], 1), jnp.stack([wide0, own0], 1)))
    share0 = shares[0, 0]

    output0, sums0 = forward(gathered0, slow_weight, residual[0], targets[0], gain)
    totals0 = jnp.sum(to_all(sums0, TP), axis=0)
    pair1 = by_half(context1, other1, hi)
    both1 = in_order(along_x(after(pair1, sums0)), x, (1, 2))
    gathered1 = laid_out(both1)
    grad0 = backward(output0, totals0, targets[0], gain)
    weight_grad0 = contract_rows(gathered0, grad0)

    pushed = ((1.0 - share0) * weight_grad0).astype(BF16)
    mass_in = shifted(leaving, REP, 2)
    pushed, mass_in = lax.optimization_barrier((pushed, mass_in))
    incoming = shifted(pushed, REP, 1)
    step0 = share0 * weight_grad0 + incoming.astype(F32)
    quotient1 = (anchor - (LR / mass1[0]) * step0).astype(BF16)
    output1, sums1 = forward(gathered1, quotient1, residual[1], targets[1], gain)
    mass2 = shares[1] * mass1 + mass_in
    mass_later = shifted(mass2, REP, -2)
    part = ((shares[1] / mass2 + (1.0 - shares[1]) / mass_later) / lax.axis_size(REP))[0]
    totals1 = jnp.sum(to_all(sums1, TP), axis=0)
    grad1 = backward(output1, totals1, targets[1], gain)
    weight_grad1 = contract_rows(gathered1, grad1)
    total = (part * (step0 + weight_grad1)).astype(BF16)

    width = total.shape[1]
    total = total.reshape(8, 4, 2, 32, width)
    kept = jnp.where(core == 0, total[:, :, 0], total[:, :, 1])
    sent = jnp.where(core == 0, total[:, :, 1], total[:, :, 0])
    total = kept.astype(F32) + shifted(sent, "core", 1).astype(F32)
    parts = jnp.transpose(total.astype(BF16), (1, 0, 2, 3))
    parts = lax.all_to_all(parts, "y", 0, 0)
    total = jnp.sum(parts.astype(F32), axis=0)
    parts = lax.all_to_all(total.astype(BF16), "z_lo", 0, 0)
    gradient = jnp.sum(parts.astype(F32), axis=0)

    anchor_rows = lax.dynamic_slice_in_dim(slow_weight, lax.axis_index(REP) * 32, 32, 0)
    new_momentum = BETA * momentum + gradient
    new_weight = anchor_rows.astype(F32) - ALPHA * LR * new_momentum
    return (new_weight, new_momentum, mass2)


def solution(mesh):
    fine = Mesh(mesh.devices.reshape(SIZES), AXES)
    return jax.shard_map(
        body,
        mesh=fine,
        in_specs=(
            P(None, REP, TP),
            P(None, REP, TP),
            P(None, REP, TP),
            P(TP),
            P(None, TP),
            P(REP, TP),
            P(None, REP),
        ),
        out_specs=(P(REP, TP), P(REP, TP), P(REP)),
        check_vma=False,
    )
```
